512 devices in a mesh: pipe: 32 (over z_lo, x), tensor: 16 (over z_hi, y, core).
Axes of the slice: x: 4, y: 4, z: 16 (z_hi: 2, z_lo: 8; z = z_hi * 8 + z_lo), core: 2. Of those that a mesh axis runs over, the one named last changes fastest.
Arguments:
- in_flight: bfloat16 [4, 4096, 7168], P(None, 'pipe', 'tensor'), may hold values from -6 to 6
- entering: bfloat16 [4, 2, 128, 7168], P(None, None, None, 'tensor'), may hold values from -6 to 6
- saved_inputs: bfloat16 [2, 2, 4096, 7168], P(None, None, 'pipe', 'tensor'), may hold values from -6 to 6
- latent_down: bfloat16 [32, 7168, 512], P('pipe', 'tensor'), may hold values from -1 to 1
- latent_back: bfloat16 [32, 512, 7168], P('pipe', None, 'tensor'), may hold values from -0.25 to 0.25
Outputs:
- section_outputs: bfloat16 [2, 2, 4096, 7168], P(None, None, 'pipe', 'tensor')
- input_grads: bfloat16 [2, 2, 4096, 7168], P(None, None, 'pipe', 'tensor')
- grad_down: bfloat16 [32, 7168, 512], P('pipe', 'tensor')
- grad_back: bfloat16 [32, 512, 7168], P('pipe', None, 'tensor')
The draws below stay inside these ranges and needn't reach their ends.
All inputs are finite; a program needn't handle non-finite values.
Results may differ from the reference program's by a relative error of at most 0.012.
Values may be sent and summed in bfloat16 or wider, within the bound.
A program may use at most 64 MiB of HBM per device.

```python
import math
import jax
import jax.numpy as jnp
from jax import lax

D = 7168
LAT = 512
TOK = 128
STEPS = 2
SECTIONS = 32
ROWS = 4096


def draw_latent_down(key, part):
    key = jax.random.fold_in(key, 11)
    values = jnp.clip(jax.random.normal(key, (SECTIONS, D, LAT), jnp.float32), -6.0, 6.0) / math.sqrt(D)
    values = jnp.clip(values, -1.0, 1.0)
    return values.astype(jnp.bfloat16)


def block_levels(own_key, extent, cuts, least, largest):
    def one(dim, shards_of):
        steps = jax.random.uniform(jax.random.fold_in(jax.random.fold_in(own_key, 6), dim), (shards_of,), jnp.float32, least / len(cuts), largest / len(cuts))
        return jnp.repeat(jnp.exp(steps), extent[dim] // shards_of).reshape((-1,) + (1,) * (len(extent) - dim - 1))

    gain = one(*cuts[0])
    for cut in cuts[1:]:
        gain = gain * one(*cut)
    return gain


def bell_draw(own_key, shape, deviation, bound, shards=(), dtype=jnp.bfloat16):
    entries = jax.random.normal(own_key, shape, jnp.float32) * deviation
    if len(shards) > 0:
        entries = block_levels(own_key, shape, shards, -0.22, 0.18) * entries
    return jnp.clip(entries, min=-bound, max=bound).astype(dtype)


def setup_inputs(seed: int = 0) -> dict:
    key_list = jax.random.split(jax.random.key(seed), 6)
    in_flight = bell_draw(key_list[0], (4, ROWS, D), 1.0, 6.0, ((1, 32), (2, 16)))
    entering = bell_draw(key_list[1], (4, STEPS, TOK, D), 1.0, 6.0, ((3, 16),))
    saved_inputs = bell_draw(key_list[2], (2, STEPS, ROWS, D), 1.0, 6.0, ((2, 32), (3, 16)))
    latent_down = draw_latent_down(jax.random.fold_in(key_list[5], 71), 0)
    latent_back = bell_draw(key_list[4], (SECTIONS, LAT, D), LAT ** -0.5, 0.25, ((0, 32), (2, 16)))
    return {"in_flight": in_flight, "entering": entering, "saved_inputs": saved_inputs, "latent_down": latent_down, "latent_back": latent_back}


eps = 1e-06

def recompute(inputs, down):
    raw = jnp.dot(inputs, down, preferred_element_type=jnp.float32)
    wide = inputs.astype(jnp.float32)
    rscale = lax.rsqrt(lax.optimization_barrier(jnp.mean(wide * wide, axis=1)) + eps)
    latent = (raw * rscale[:, None]).astype(jnp.bfloat16)
    scores = jnp.dot(latent, latent.T, preferred_element_type=jnp.float32) * (4.0 / LAT)
    rows = lax.broadcasted_iota(jnp.int32, scores.shape, 0)
    cols = lax.broadcasted_iota(jnp.int32, scores.shape, 1)
    scores = jnp.where(rows >= cols, scores, -jnp.inf)
    probs = jax.nn.softmax(scores, axis=1)
    probs_b = probs.astype(jnp.bfloat16)
    mixed = jnp.dot(probs_b, latent, preferred_element_type=jnp.float32).astype(jnp.bfloat16)
    return (raw, wide, rscale, latent, probs, probs_b, mixed)

def section_forward(inputs, down, back):
    raw, wide, rscale, latent, probs, probs_b, mixed = recompute(inputs, down)
    return (wide + jnp.dot(mixed, back, preferred_element_type=jnp.float32)).astype(jnp.bfloat16)

def section_backward(inputs, cotangent, down, back):
    raw, wide, rscale, latent, probs, probs_b, mixed = recompute(inputs, down)
    grad_back = jnp.dot(mixed.T, cotangent, preferred_element_type=jnp.float32)
    dmixed = jnp.dot(cotangent, back.T, preferred_element_type=jnp.float32).astype(jnp.bfloat16)
    dprobs = jnp.dot(dmixed, latent.T, preferred_element_type=jnp.float32)
    dscores = probs * (dprobs - lax.optimization_barrier(jnp.sum(probs * dprobs, axis=1, keepdims=True)))
    dsym = ((dscores + dscores.T) * (4.0 / LAT)).astype(jnp.bfloat16)
    dlatent = jnp.dot(dsym, latent, preferred_element_type=jnp.float32) + jnp.dot(probs_b.T, dmixed, preferred_element_type=jnp.float32)
    draw = (dlatent * rscale[:, None]).astype(jnp.bfloat16)
    grad_down = jnp.dot(inputs.T, draw, preferred_element_type=jnp.float32)
    dscale = lax.optimization_barrier(jnp.sum(dlatent * raw, axis=1))
    result = cotangent.astype(jnp.float32) + jnp.dot(draw, down.T, preferred_element_type=jnp.float32)
    result = result - wide * (rscale * rscale * rscale * dscale / D)[:, None]
    return (result.astype(jnp.bfloat16), grad_down, grad_back)

def combine(first, second):
    first_b, second_b = lax.optimization_barrier((first.astype(jnp.bfloat16), second.astype(jnp.bfloat16)))
    return (first_b.astype(jnp.float32) + second_b.astype(jnp.float32)).astype(jnp.bfloat16)

def reference(in_flight, entering, saved_inputs, latent_down, latent_back):
    sections = latent_down.shape[0]
    forward = jax.vmap(section_forward)
    backward = jax.vmap(section_backward)

    def split(rows):
        return rows.reshape(sections, TOK, D)
    east_act, west_act, east_grad, west_grad = [split(in_flight[k]) for k in range(4)]
    down_rev = latent_down[::-1]
    back_rev = latent_back[::-1]
    sum_down_east = jnp.zeros(latent_down.shape, jnp.float32)
    sum_down_west = jnp.zeros(latent_down.shape, jnp.float32)
    sum_back_east = jnp.zeros(latent_back.shape, jnp.float32)
    sum_back_west = jnp.zeros(latent_back.shape, jnp.float32)
    outs_east, outs_west, grads_east, grads_west = ([], [], [], [])
    for step in range(STEPS):
        east_in = jnp.concatenate([entering[0, step][None], east_act[:-1]], axis=0)
        west_cot = jnp.concatenate([entering[3, step][None], west_grad[:-1]], axis=0)
        west_in = jnp.concatenate([west_act[1:], entering[1, step][None]], axis=0)
        east_cot = jnp.concatenate([east_grad[1:], entering[2, step][None]], axis=0)
        east_act = forward(east_in, latent_down, latent_back)
        west_act = forward(west_in, down_rev, back_rev)
        east_grad, part_down, part_back = backward(split(saved_inputs[0, step]), east_cot, latent_down, latent_back)
        sum_down_east = sum_down_east + part_down
        sum_back_east = sum_back_east + part_back
        west_grad, part_down, part_back = backward(split(saved_inputs[1, step]), west_cot, down_rev, back_rev)
        sum_down_west = sum_down_west + part_down
        sum_back_west = sum_back_west + part_back
        outs_east.append(east_act.reshape(sections * TOK, D))
        outs_west.append(west_act.reshape(sections * TOK, D))
        grads_east.append(east_grad.reshape(sections * TOK, D))
        grads_west.append(west_grad.reshape(sections * TOK, D))
    section_outputs = jnp.stack([jnp.stack(outs_east), jnp.stack(outs_west)])
    input_grads = jnp.stack([jnp.stack(grads_east), jnp.stack(grads_west)])
    grad_down = combine(sum_down_east, sum_down_west[::-1])
    grad_back = combine(sum_back_east, sum_back_west[::-1])
    return (section_outputs, input_grads, grad_down, grad_back)
```

```python
import functools

import jax
import jax.numpy as jnp
from jax import lax
from jax.experimental import pallas as pl
from jax.experimental.pallas import tpu as pltpu
from jax.sharding import PartitionSpec as P

MESH = pl.DeviceIdType.MESH
TOK = 128
LAT = 512
LANES = 128
BLOCKS = LAT // LANES
eps = 1e-06
F32 = jnp.float32
BF16 = jnp.bfloat16

ROUNDS = {
    "a0": ("raw", "saved", "saved", "dm"),
    "b0": ("dm", "saved"),
    "b1": ("raw", "saved"),
    "a1": ("raw", "dm"),
    "b2": ("dm",),
    "b3": ("raw",),
}


def blocks_out(kinds):
    return BLOCKS * len(kinds) + (any(k != "dm" for k in kinds))


def blocks_back(kinds):
    return BLOCKS * len(kinds) + ("saved" in kinds)


def lane_pair(values, shape):
    lane = lax.broadcasted_iota(jnp.int32, shape, 1)
    block = jnp.zeros(shape, F32)
    for q, value in enumerate(values):
        high = value.astype(BF16).astype(F32)
        block = jnp.where(lane == 2 * q, high, jnp.where(lane == 2 * q + 1, value - high, block))
    return block.astype(BF16)


def from_pair(block, q):
    lane = lax.broadcasted_iota(jnp.int32, block.shape, 1)
    mine = (lane == 2 * q) | (lane == 2 * q + 1)
    return jnp.sum(jnp.where(mine, block, 0.0), axis=1, keepdims=True)


def dot(a, b, over=((1,), (0,))):
    return lax.dot_general(a, b, (over, ((), ())), preferred_element_type=F32)


NT = ((1,), (1,))
TN = ((0,), (0,))


def attend(latent):
    scores = dot(latent, latent, NT) * (4.0 / LAT)
    rows = lax.broadcasted_iota(jnp.int32, scores.shape, 0)
    cols = lax.broadcasted_iota(jnp.int32, scores.shape, 1)
    scores = jnp.where(rows >= cols, scores, -jnp.inf)
    top = jnp.max(scores, axis=1, keepdims=True)
    weights = jnp.exp(scores - top)
    probs = weights / jnp.sum(weights, axis=1, keepdims=True)
    probs_b = probs.astype(BF16)
    return probs, probs_b, dot(probs_b, latent).astype(BF16)


class Semaphores:
    def __init__(self, ref):
        self.ref, self.used = ref, 0

    def new(self):
        self.used += 1
        return self.ref.at[self.used - 1]


N_LOCAL, N_REMOTE = 48, 160


class Round:
    def __init__(self, kinds, refs, remote, mesh_at, width):
        self.kinds, self.width = kinds, width
        self.send, self.got, self.mine, self.other, self.full = refs
        self.pipe, self.half, self.j, self.group = mesh_at
        self.rows = TOK // self.group
        j, group = self.j, self.group
        self.own = pl.ds(pl.multiple_of(j * self.rows, self.rows), self.rows)
        self.scatter, self.gather, self.arrive = [], [], []
        for k in range(1, group):
            to = lax.rem(j + k, group)
            source = lax.rem(j - k + group, group)
            to_rows = pl.ds(pl.multiple_of(to * self.rows, self.rows), self.rows)
            from_rows = pl.ds(pl.multiple_of(source * self.rows, self.rows), self.rows)
            device = (self.pipe, self.half * group + to)
            self.scatter.append(remote(self.send.at[:, to_rows, :], self.got.at[k - 1], device))
            out = remote(self.full.at[:, self.own, :], self.full.at[:, self.own, :], device)
            self.gather.append(out)
            self.arrive.append(
                pltpu.make_async_remote_copy(
                    src_ref=self.full.at[:, from_rows, :],
                    dst_ref=self.full.at[:, from_rows, :],
                    send_sem=out.src_sem,
                    recv_sem=out.dst_sem,
                    device_id=device,
                    device_id_type=MESH,
                )
            )
        self.swap = remote(self.mine, self.other, (self.pipe, (1 - self.half) * group + j))

    def start(self, parts):
        norms = []
        for p, (value, norm) in enumerate(parts):
            for c in range(BLOCKS):
                self.send[p * BLOCKS + c] = value[:, c * LANES : (c + 1) * LANES].astype(BF16)
            if norm is not None:
                norms.append(norm)
        if norms:
            self.send[len(parts) * BLOCKS] = lane_pair(norms, (TOK, LANES))
        for copy in self.scatter:
            copy.start()

    def half_sum(self):
        for copy in self.scatter:
            copy.wait_recv()
        total = self.send[:, self.own, :].astype(F32)
        for k in range(self.group - 1):
            total = total + self.got[k].astype(F32)
        last = len(self.kinds) * BLOCKS
        self.mine[:last] = total[:last].astype(BF16)
        if blocks_out(self.kinds) > last:
            norms = [from_pair(total[last], q) for q in range(sum(k != "dm" for k in self.kinds))]
            self.mine[last] = lane_pair(norms, (self.rows, LANES))
        self.swap.start()

    def finish(self):
        self.swap.wait_recv()
        total = self.mine[...].astype(F32) + self.other[...].astype(F32)
        last = len(self.kinds) * BLOCKS
        raws, scales = 0, []
        for p, kind in enumerate(self.kinds):
            value = total[p * BLOCKS : (p + 1) * BLOCKS]
            if kind != "dm":
                scale = lax.rsqrt(from_pair(total[last], raws) / self.width + eps)
                raws += 1
                value = value * scale[None]
                if kind == "saved":
                    scales.append(scale)
            self.full[p * BLOCKS : (p + 1) * BLOCKS, self.own, :] = value.astype(BF16)
        if scales:
            self.full[last, self.own, :] = lane_pair(scales, (self.rows, LANES))
        for copy in self.gather:
            copy.start()

    def collect(self):
        for copy in self.arrive:
            copy.wait_recv()

    def part(self, p):
        return jnp.concatenate([self.full[p * BLOCKS + c] for c in range(BLOCKS)], axis=1)

    def scale(self, q):
        return from_pair(self.full[len(self.kinds) * BLOCKS].astype(F32), q)

    def drain(self):
        for copy in self.scatter + self.gather + [self.swap]:
            copy.wait_send()


def kernel(sections, shards, *refs):
    in_flight, entering, saved, down_in, back_in, outs, grads, g_down, g_back = refs[:9]
    down, back, xs, dys, kept, fs, gs, draws, mixes, sum_down, sum_back = refs[9:20]
    ssem, rsem, lsem = refs[-3:]
    buffers = refs[20:-3]
    group = shards // 2
    width = down.shape[0] * shards

    me = lax.axis_index("pipe")
    place = lax.axis_index("tensor")
    half, j = place // group, lax.rem(place, group)
    last = sections - 1
    sends, receives, locals_ = Semaphores(ssem), Semaphores(rsem), Semaphores(lsem)

    def remote(source, target, device):
        return pltpu.make_async_remote_copy(
            src_ref=source,
            dst_ref=target,
            send_sem=sends.new(),
            recv_sem=receives.new(),
            device_id=device,
            device_id_type=MESH,
        )

    def local(source, target):
        return pltpu.make_async_copy(source, target, locals_.new())

    not_first, not_last = me > 0, me < last
    nxt = (jnp.minimum(me + 1, last), place)
    prev = (jnp.maximum(me - 1, 0), place)
    across = (last - me, place)
    x_self, dy_self = me == sections // 2, me == sections // 2 - 1
    x_far = not_first & jnp.logical_not(x_self)
    dy_far = not_last & jnp.logical_not(dy_self)
    x_to = (jnp.where(x_far, sections - me, 0), place)
    dy_to = (jnp.where(dy_far, last - 1 - me, 0), place)

    load_down, load_back = local(down_in.at[0], down), local(back_in.at[0], back)
    load_kept = [local(saved.at[0, t], kept.at[0, t]) for t in range(2)]
    for copy in [load_down, load_back] + load_kept:
        copy.start()
    load_x = [local(entering.at[s, t], xs.at[s, t]) for s in range(2) for t in range(2)]
    load_dy = [local(entering.at[2 + s, t], dys.at[s, t]) for s in range(2) for t in range(2)]
    load_x_self = local(in_flight.at[1], xs.at[1, 0])
    load_dy_self = local(in_flight.at[3], dys.at[1, 0])

    def when_all(condition, copies, what):
        @pl.when(condition)
        def _():
            for copy in copies:
                getattr(copy, what)()

    when_all(me == 0, load_x, "start")
    when_all(me == last, load_dy, "start")
    when_all(x_self, [load_x_self], "start")
    when_all(dy_self, [load_dy_self], "start")

    barrier = pltpu.get_barrier_semaphore()

    def greet(device):
        pl.semaphore_signal(barrier, inc=1, device_id=device, device_id_type=MESH)

    for k in range(1, group):
        greet((me, half * group + lax.rem(j + k, group)))
    greet((me, (1 - half) * group + j))
    greet(across)
    count = group + 1
    for condition, device in ((not_last, nxt), (not_first, prev), (x_far, x_to), (dy_far, dy_to)):
        pl.when(condition)(functools.partial(greet, device))
        count = count + condition.astype(jnp.int32)
    pl.semaphore_wait(barrier, count)

    send_xa = remote(in_flight.at[0], xs.at[0, 0], nxt)
    send_dya = remote(in_flight.at[2], dys.at[0, 0], prev)
    send_dyb = remote(in_flight.at[3], dys.at[1, 0], dy_to)
    send_kept = [remote(saved.at[1, t], kept.at[1, t], across) for t in range(2)]
    send_xb = remote(in_flight.at[1], xs.at[1, 0], x_to)
    when_all(not_last, [send_xa], "start")
    when_all(not_first, [send_dya], "start")
    when_all(dy_far, [send_dyb], "start")
    send_kept[0].start()

    at = (me, half, j, group)
    rounds = {}
    for n, (name, kinds) in enumerate(ROUNDS.items()):
        rounds[name] = Round(kinds, buffers[5 * n : 5 * n + 5], remote, at, width)

    def raw_part(x):
        wide = x.astype(F32)
        return dot(x, down[...]), jnp.sum(wide * wide, axis=1, keepdims=True)

    def dm_part(dy):
        return dot(dy, back[...], NT), None

    def forward(x, mixed, slot):
        slot[...] = (x.astype(F32) + dot(mixed, back[...])).astype(BF16)

    def backward(s, t, saved_state, dmixed):
        latent, scale, probs, probs_b = saved_state
        dprobs = dot(dmixed, latent, NT)
        dscores = probs * (dprobs - jnp.sum(probs * dprobs, axis=1, keepdims=True))
        dsym = ((dscores + dscores.T) * (4.0 / LAT)).astype(BF16)
        dlatent = dot(dsym, latent) + dot(probs_b, dmixed, TN)
        draw = (dlatent * scale).astype(BF16)
        draws[s, t] = draw
        along = jnp.sum(dlatent * latent.astype(F32), axis=1, keepdims=True)
        result = dys[s, t].astype(F32) + dot(draw, down[...], NT)
        result = result - kept[s, t].astype(F32) * (scale * scale * along / width)
        gs[s, t] = result.astype(BF16)

    def recompute(s, t, latent, scale):
        probs, probs_b, mixed = attend(latent)
        mixes[s, t] = mixed
        return latent, scale, probs, probs_b

    def stream_grads(s):
        rows = (2 * TOK, LAT)
        cols = (2 * TOK, down.shape[0])
        return (
            dot(kept[s].reshape(cols), draws[s].reshape(rows), TN),
            dot(mixes[s].reshape(rows), dys[s].reshape(cols), TN),
        )

    shift_x = [remote(fs.at[s, 0], xs.at[s, 1], nxt) for s in range(2)]
    shift_dy = [remote(gs.at[s, 0], dys.at[s, 1], prev) for s in range(2)]
    out_f = [remote(fs.at[1, t], outs.at[1, t], across) for t in range(2)]
    out_g = [remote(gs.at[1, t], grads.at[1, t], across) for t in range(2)]
    keep_f = [local(fs.at[0, t], outs.at[0, t]) for t in range(2)]
    keep_g = [local(gs.at[0, t], grads.at[0, t]) for t in range(2)]

    load_down.wait()
    for copy in load_kept:
        copy.wait()
    parts = [raw_part(kept[0, t]) for t in range(2)]
    load_back.wait()
    when_all(me == 0, load_x, "wait")
    when_all(me == last, load_dy, "wait")
    when_all(x_self, [load_x_self], "wait")
    when_all(dy_self, [load_dy_self], "wait")
    when_all(not_first, [send_xa], "wait_recv")
    when_all(not_last, [send_dya], "wait_recv")
    rounds["a0"].start([raw_part(xs[0, 0])] + parts + [dm_part(dys[0, 0])])
    rounds["a0"].half_sum()

    when_all(dy_far, [send_dyb], "wait_recv")
    send_kept[0].wait_recv()
    when_all(x_far, [send_xb], "start")
    send_kept[1].start()
    rounds["b0"].start([dm_part(dys[1, 0]), raw_part(kept[1, 0])])
    rounds["a0"].finish()
    rounds["b0"].half_sum()

    rounds["a0"].collect()
    part = rounds["a0"].part
    forward(xs[0, 0], attend(part(0))[2], fs.at[0, 0])
    when_all(not_last, [shift_x[0]], "start")
    state = recompute(0, 0, part(1), rounds["a0"].scale(0))
    backward(0, 0, state, part(3))
    when_all(not_first, [shift_dy[0]], "start")
    keep_f[0].start()
    keep_g[0].start()
    state_a = recompute(0, 1, part(2), rounds["a0"].scale(1))

    when_all(not_first, [shift_x[0]], "wait_recv")
    when_all(not_last, [shift_dy[0]], "wait_recv")
    rounds["a1"].start([raw_part(xs[0, 1]), dm_part(dys[0, 1])])
    rounds["b0"].finish()
    rounds["a1"].half_sum()

    rounds["b0"].collect()
    state = recompute(1, 0, rounds["b0"].part(1), rounds["b0"].scale(0))
    backward(1, 0, state, rounds["b0"].part(0))
    when_all(not_first, [shift_dy[1]], "start")
    out_g[0].start()

    when_all(x_far, [send_xb], "wait_recv")
    send_kept[1].wait_recv()
    rounds["b1"].start([raw_part(xs[1, 0]), raw_part(kept[1, 1])])
    when_all(not_last, [shift_dy[1]], "wait_recv")
    rounds["b2"].start([dm_part(dys[1, 1])])
    rounds["b1"].half_sum()
    rounds["b2"].half_sum()

    rounds["a1"].finish()
    rounds["a1"].collect()
    forward(xs[0, 1], attend(rounds["a1"].part(0))[2], fs.at[0, 1])
    backward(0, 1, state_a, rounds["a1"].part(1))
    keep_f[1].start()
    keep_g[1].start()

    rounds["b1"].finish()
    rounds["b2"].finish()
    rounds["b1"].collect()
    forward(xs[1, 0], attend(rounds["b1"].part(0))[2], fs.at[1, 0])
    when_all(not_last, [shift_x[1]], "start")
    out_f[0].start()
    state_b = recompute(1, 1, rounds["b1"].part(1), rounds["b1"].scale(0))
    rounds["b2"].collect()
    backward(1, 1, state_b, rounds["b2"].part(0))
    out_g[1].start()
    when_all(not_first, [shift_x[1]], "wait_recv")
    rounds["b3"].start([raw_part(xs[1, 1])])
    rounds["b3"].half_sum()

    own, far = stream_grads(0), stream_grads(1)
    for target, first, second in zip((sum_down, sum_back), own, far, strict=True):
        target[...] = (first.astype(BF16).astype(F32) + second.astype(BF16).astype(F32)).astype(BF16)
    keep_down, keep_back = local(sum_down, g_down.at[0]), local(sum_back, g_back.at[0])
    keep_down.start()
    keep_back.start()

    rounds["b3"].finish()
    rounds["b3"].collect()
    forward(xs[1, 1], attend(rounds["b3"].part(0))[2], fs.at[1, 1])
    out_f[1].start()

    for copy in keep_f + keep_g + [keep_down, keep_back]:
        copy.wait()
    for copy in out_f + out_g:
        copy.wait()
    for copy in send_kept:
        copy.wait_send()
    for item in rounds.values():
        item.drain()
    when_all(not_last, [send_xa] + shift_x, "wait_send")
    when_all(not_first, [send_dya] + shift_dy, "wait_send")
    when_all(x_far, [send_xb], "wait_send")
    when_all(dy_far, [send_dyb], "wait_send")


def solution(mesh):
    sections, shards = mesh.shape["pipe"], mesh.shape["tensor"]
    group = shards // 2
    rows = TOK // group

    def step(in_flight, entering, saved_inputs, latent_down, latent_back):
        local = latent_down.shape[1]
        act = pltpu.VMEM((2, 2, TOK, local), BF16)
        state = pltpu.VMEM((2, 2, TOK, LAT), BF16)
        buffers = []
        for kinds in ROUNDS.values():
            sent, returned = blocks_out(kinds), blocks_back(kinds)
            buffers += [
                pltpu.VMEM((sent, TOK, LANES), BF16),
                pltpu.VMEM((group - 1, sent, rows, LANES), BF16),
                pltpu.VMEM((sent, rows, LANES), BF16),
                pltpu.VMEM((sent, rows, LANES), BF16),
                pltpu.VMEM((returned, TOK, LANES), BF16),
            ]
        anywhere = pl.BlockSpec(memory_space=pl.ANY)
        return pl.pallas_call(
            functools.partial(kernel, sections, shards),
            out_shape=(
                jax.ShapeDtypeStruct((2, 2, TOK, local), BF16),
                jax.ShapeDtypeStruct((2, 2, TOK, local), BF16),
                jax.ShapeDtypeStruct((1, local, LAT), BF16),
                jax.ShapeDtypeStruct((1, LAT, local), BF16),
            ),
            in_specs=[anywhere] * 5,
            out_specs=[anywhere] * 4,
            scratch_shapes=[
                pltpu.VMEM((local, LAT), BF16),
                pltpu.VMEM((LAT, local), BF16),
                *[act] * 5,
                *[state] * 2,
                pltpu.VMEM((local, LAT), BF16),
                pltpu.VMEM((LAT, local), BF16),
                *buffers,
                pltpu.SemaphoreType.DMA((N_REMOTE,)),
                pltpu.SemaphoreType.DMA((N_REMOTE,)),
                pltpu.SemaphoreType.DMA((N_LOCAL,)),
            ],
            compiler_params=pltpu.CompilerParams(
                collective_id=0, has_side_effects=True, vmem_limit_bytes=40 * 2**20
            ),
        )(in_flight, entering, saved_inputs, latent_down, latent_back)

    return jax.shard_map(
        step,
        mesh=mesh,
        in_specs=(
            P(None, "pipe", "tensor"),
            P(None, None, None, "tensor"),
            P(None, None, "pipe", "tensor"),
            P("pipe", "tensor", None),
            P("pipe", None, "tensor"),
        ),
        out_specs=(
            P(None, None, "pipe", "tensor"),
            P(None, None, "pipe", "tensor"),
            P("pipe", "tensor", None),
            P("pipe", None, "tensor"),
        ),
        check_vma=False,
    )
```

```python
import functools

import jax
import jax.numpy as jnp
from jax import lax
from jax.experimental import pallas as pl
from jax.experimental.pallas import tpu as pltpu
from jax.sharding import PartitionSpec as P


MESH = pl.DeviceIdType.MESH
TOK = 128
LAT = 512
NORM_ROWS = 16
eps = 1e-06
F32 = jnp.float32
BF16 = jnp.bfloat16
NN = ((1,), (0,))
NT = ((1,), (1,))
TN = ((0,), (0,))

ROUNDS = {
    "a0": ("raw", "raw", "dm"),
    "b0": ("raw", "raw", "dm"),
    "a1": ("raw", "raw", "dm"),
    "b1": ("raw", "raw", "dm"),
}
N_LOCAL, N_REMOTE = 48, 160

(
    ENTERED, A0_HERE, A0_SCATTERED, A0_SWAPPED, A0_GATHERED, A0_DONE, B0_SCATTERED, B0_SWAPPED,
    B0_GATHERED, B0_COLLECTED, B0_DONE, A1_SCATTERED, B1_HERE, B1_SCATTERED, B1_SWAPPED,
    B1_GATHERED, B1_COLLECTED, F1_DONE, B1_DONE,
) = range(19)
SCHEDULE = {
    "in": (ENTERED, A0_SWAPPED, A0_SWAPPED, A0_SWAPPED),
    "kept": (ENTERED, B0_GATHERED, B0_GATHERED, B0_GATHERED),
    "f0": (A1_SCATTERED, B1_SCATTERED, B1_SCATTERED, B1_SCATTERED),
    "g0": (B1_COLLECTED, B1_COLLECTED, B1_COLLECTED, B1_COLLECTED),
    "f1": (F1_DONE, F1_DONE, F1_DONE, F1_DONE),
    "g1": (B1_DONE, B1_DONE, B1_DONE, B1_DONE),
}


def due(item, off, n):
    classes = [c for c, start in enumerate(SCHEDULE[item]) if start == n]
    if not classes:
        return None
    now = off == classes[0]
    for c in classes[1:]:
        now = now | (off == c)
    return now


def chunk_rows(kinds, rows):
    return rows * len(kinds) + NORM_ROWS * ("raw" in kinds)


def dot(a, b, over=NN):
    return lax.dot_general(a, b, (over, ((), ())), preferred_element_type=F32)


def norm_block(norms):
    row = lax.broadcasted_iota(jnp.int32, (NORM_ROWS, TOK), 0)
    block = jnp.zeros((NORM_ROWS, TOK), F32)
    for q, value in enumerate(norms):
        high = value.astype(BF16).astype(F32)
        block = jnp.where(row == 2 * q, high, jnp.where(row == 2 * q + 1, value - high, block))
    return block.astype(BF16)


def norms_of(block, count):
    return [block[2 * q : 2 * q + 1] + block[2 * q + 1 : 2 * q + 2] for q in range(count)]


def attend(latent):
    scores = dot(latent, latent, TN) * (4.0 / LAT)
    key = lax.broadcasted_iota(jnp.int32, scores.shape, 0)
    query = lax.broadcasted_iota(jnp.int32, scores.shape, 1)
    scores = jnp.where(query >= key, scores, -jnp.inf)
    weights = jnp.exp(scores - jnp.max(scores, axis=0, keepdims=True))
    probs = weights / jnp.sum(weights, axis=0, keepdims=True)
    probs_b = probs.astype(BF16)
    return probs, probs_b, dot(latent, probs_b).astype(BF16)


class Semaphores:
    def __init__(self, ref):
        self.ref, self.used = ref, 0

    def new(self):
        self.used += 1
        return self.ref.at[self.used - 1]


class Round:
    def __init__(self, kinds, refs, remote, mesh_at, width):
        self.kinds, self.width = kinds, width
        self.send, self.got, self.mine, self.other, self.full = refs
        self.pipe, self.half, self.j, self.group = mesh_at
        self.rows = LAT // self.group
        self.raws = sum(k == "raw" for k in kinds)
        j, group = self.j, self.group
        own = pl.ds(pl.multiple_of(j * self.rows, self.rows), self.rows)
        self.own = own
        self.scatter, self.gather, self.arrive = [], [], []
        for k in range(1, group):
            to = lax.rem(j + k, group)
            source = lax.rem(j - k + group, group)
            theirs = pl.ds(pl.multiple_of(source * self.rows, self.rows), self.rows)
            device = (self.pipe, self.half * group + to)
            self.scatter.append(remote(self.send.at[to], self.got.at[k - 1], device))
            out = remote(self.full.at[:, own, :], self.full.at[:, own, :], device)
            self.gather.append(out)
            self.arrive.append(
                pltpu.make_async_remote_copy(
                    src_ref=self.full.at[:, theirs, :],
                    dst_ref=self.full.at[:, theirs, :],
                    send_sem=out.src_sem,
                    recv_sem=out.dst_sem,
                    device_id=device,
                    device_id_type=MESH,
                )
            )
        self.swap = remote(self.mine, self.other, (self.pipe, (1 - self.half) * group + j))

    def start(self, parts):
        rows = self.rows
        norms = [norm for _, norm in parts if norm is not None]
        for p, (value, _) in enumerate(parts):
            value = value.astype(BF16)
            for g in range(self.group):
                self.send[g, p * rows : (p + 1) * rows] = value[g * rows : (g + 1) * rows]
        if norms:
            block = norm_block(norms)
            for g in range(self.group):
                self.send[g, len(parts) * rows :] = block
        for copy in self.scatter:
            copy.start()

    def half_sum(self):
        for copy in self.scatter:
            copy.wait_recv()
        total = self.send[self.j].astype(F32)
        for k in range(self.group - 1):
            total = total + self.got[k].astype(F32)
        last = len(self.kinds) * self.rows
        self.mine[:last] = total[:last].astype(BF16)
        if self.raws:
            self.mine[last:] = norm_block(norms_of(total[last:], self.raws))
        self.swap.start()

    def finish(self):
        self.swap.wait_recv()
        total = self.mine[...].astype(F32) + self.other[...].astype(F32)
        rows = self.rows
        scales, raw = self.scales_of(total), 0
        for p, kind in enumerate(self.kinds):
            value = total[p * rows : (p + 1) * rows]
            if kind == "raw":
                value = value * scales[raw]
                raw += 1
            self.full[p, self.own, :] = value.astype(BF16)
        for copy in self.gather:
            copy.start()

    def scales_of(self, total):
        norms = norms_of(total[len(self.kinds) * self.rows :], self.raws) if self.raws else []
        return [lax.rsqrt(norm / self.width + eps) for norm in norms]

    @property
    def scales(self):
        return self.scales_of(self.mine[...].astype(F32) + self.other[...].astype(F32))

    def collect(self):
        for copy in self.arrive:
            copy.wait_recv()

    def part(self, p):
        return self.full[p]

    def drain(self):
        for copy in self.scatter + self.gather + [self.swap]:
            copy.wait_send()


def kernel(sections, shards, *refs):
    in_flight, entering, saved, down_in, back_in, outs, grads, g_down, g_back = refs[:9]
    down, back, down_t, back_t, xs, dys, kept, fs, gs, draws, mixes, sum_down, sum_back = refs[9:22]
    ssem, rsem, lsem = refs[-3:]
    buffers = refs[22:-3]
    group = shards // 2
    width = down.shape[0] * shards

    me = lax.axis_index("pipe")
    place = lax.axis_index("tensor")
    half, j = place // group, lax.rem(place, group)
    last = sections - 1
    sends, receives, locals_ = Semaphores(ssem), Semaphores(rsem), Semaphores(lsem)

    def remote(source, target, device):
        return pltpu.make_async_remote_copy(
            src_ref=source,
            dst_ref=target,
            send_sem=sends.new(),
            recv_sem=receives.new(),
            device_id=device,
            device_id_type=MESH,
        )

    def local(source, target):
        return pltpu.make_async_copy(source, target, locals_.new())

    not_first, not_last = me > 0, me < last
    nxt = (jnp.minimum(me + 1, last), place)
    prev = (jnp.maximum(me - 1, 0), place)
    across = (last - me, place)
    x_self, dy_self = me == sections // 2, me == sections // 2 - 1
    x_far = not_first & jnp.logical_not(x_self)
    dy_far = not_last & jnp.logical_not(dy_self)
    x_to = (jnp.where(x_far, sections - me, 0), place)
    dy_to = (jnp.where(dy_far, last - 1 - me, 0), place)

    load_down, load_back = local(down_in.at[0], down), local(back_in.at[0], back)
    load_kept = [local(saved.at[0, t], kept.at[0, t]) for t in range(2)]
    for copy in [load_down, load_back] + load_kept:
        copy.start()
    load_x = [local(entering.at[s, t], xs.at[s, t]) for s in range(2) for t in range(2)]
    load_dy = [local(entering.at[2 + s, t], dys.at[s, t]) for s in range(2) for t in range(2)]
    load_x_self = local(in_flight.at[1], xs.at[1, 0])
    load_dy_self = local(in_flight.at[3], dys.at[1, 0])

    def when_all(condition, copies, what):
        @pl.when(condition)
        def _():
            for copy in copies:
                getattr(copy, what)()

    when_all(me == 0, load_x, "start")
    when_all(me == last, load_dy, "start")
    when_all(x_self, [load_x_self], "start")
    when_all(dy_self, [load_dy_self], "start")

    def raw_part(x):
        wide = x.astype(F32)
        return dot(down_t[...], x), jnp.sum(wide * wide, axis=0, keepdims=True)

    barrier = pltpu.get_barrier_semaphore()

    def greet(device):
        pl.semaphore_signal(barrier, inc=1, device_id=device, device_id_type=MESH)

    for k in range(1, group):
        greet((me, half * group + lax.rem(j + k, group)))
    greet((me, (1 - half) * group + j))
    greet(across)
    count = group + 1
    for condition, device in ((not_last, nxt), (not_first, prev), (x_far, x_to), (dy_far, dy_to)):
        pl.when(condition)(functools.partial(greet, device))
        count = count + condition.astype(jnp.int32)
    load_down.wait()
    load_back.wait()
    down_t[...] = down[...].T
    back_t[...] = back[...].T
    for copy in load_kept:
        copy.wait()
    kept_parts = [raw_part(kept[0, t]) for t in range(2)]
    when_all(me == 0, load_x, "wait")
    when_all(me == last, load_dy, "wait")
    when_all(x_self, [load_x_self], "wait")
    when_all(dy_self, [load_dy_self], "wait")
    pl.semaphore_wait(barrier, count)

    send_xa = remote(in_flight.at[0], xs.at[0, 0], nxt)
    send_dya = remote(in_flight.at[2], dys.at[0, 0], prev)
    send_dyb = remote(in_flight.at[3], dys.at[1, 0], dy_to)
    send_kept = [remote(saved.at[1, t], kept.at[1, t], across) for t in range(2)]
    send_xb = remote(in_flight.at[1], xs.at[1, 0], x_to)
    when_all(not_last, [send_xa], "start")
    when_all(not_first, [send_dya], "start")
    at = (me, half, j, group)
    rounds = {}
    for n, (name, kinds) in enumerate(ROUNDS.items()):
        rounds[name] = Round(kinds, buffers[5 * n : 5 * n + 5], remote, at, width)

    def dm_part(dy):
        return dot(back_t[...], dy), None

    def forward(x, mixed, slot):
        slot[...] = (x.astype(F32) + dot(back[...], mixed)).astype(BF16)

    def backward(s, t, state, dmixed):
        latent, scale, probs, probs_b = state
        dprobs = dot(latent, dmixed, TN)
        dscores = probs * (dprobs - jnp.sum(probs * dprobs, axis=0, keepdims=True))
        dsym = ((dscores + dscores.T) * (4.0 / LAT)).astype(BF16)
        dlatent = dot(latent, dsym) + dot(dmixed, probs_b, NT)
        draw = (dlatent * scale).astype(BF16)
        draws[s, t] = draw
        along = jnp.sum(dlatent * latent.astype(F32), axis=0, keepdims=True)
        result = dys[s, t].astype(F32) + dot(down[...], draw)
        result = result - kept[s, t].astype(F32) * (scale * scale * along / width)
        gs[s, t] = result.astype(BF16)

    def recompute(s, t, latent, scale):
        probs, probs_b, mixed = attend(latent)
        mixes[s, t] = mixed
        return latent, scale, probs, probs_b

    def add_grads(s):
        for target, left, right in ((sum_down, kept, draws), (sum_back, dys, mixes)):
            total = dot(left[s, 0], right[s, 0], NT) + dot(left[s, 1], right[s, 1], NT)
            total = total.astype(BF16)
            if s == 1:
                total = (target[...].astype(F32) + total.astype(F32)).astype(BF16)
            target[...] = total

    shift_x = [remote(fs.at[s, 0], xs.at[s, 1], nxt) for s in range(2)]
    shift_dy = [remote(gs.at[s, 0], dys.at[s, 1], prev) for s in range(2)]
    out_f = [remote(fs.at[1, t], outs.at[1, t], across) for t in range(2)]
    out_g = [remote(gs.at[1, t], grads.at[1, t], across) for t in range(2)]
    keep_f = [local(fs.at[0, t], outs.at[0, t]) for t in range(2)]
    keep_g = [local(gs.at[0, t], grads.at[0, t]) for t in range(2)]

    off = jnp.where(me < sections // 2, sections // 2 - 1 - me, me - sections // 2) // max(sections // 8, 1)

    everyone = [(None, copy) for copy in send_kept]
    bulk = {
        "in": [(x_far, send_xb), (dy_far, send_dyb), everyone[0]],
        "kept": [everyone[1]],
        "f0": [(None, out_f[0])],
        "g0": [(None, out_g[0])],
        "f1": [(None, out_f[1])],
        "g1": [(None, out_g[1])],
    }

    def point(n):
        for item, copies in bulk.items():
            now = due(item, off, n)
            if now is None:
                continue

            @pl.when(now)
            def _():
                for condition, copy in copies:
                    if condition is None:
                        copy.start()
                    else:
                        when_all(condition, [copy], "start")

    a0, b0, a1, b1 = (rounds[name] for name in ROUNDS)

    def take_b0():
        when_all(x_far, [send_xb], "wait_recv")
        when_all(dy_far, [send_dyb], "wait_recv")
        send_kept[0].wait_recv()
        b0.start([raw_part(xs[1, 0]), raw_part(kept[1, 0]), dm_part(dys[1, 0])])
        point(B0_SCATTERED)

    point(ENTERED)
    when_all(not_first, [send_xa], "wait_recv")
    when_all(not_last, [send_dya], "wait_recv")
    point(A0_HERE)
    a0.start([raw_part(xs[0, 0]), kept_parts[0], dm_part(dys[0, 0])])
    point(A0_SCATTERED)
    a0.half_sum()
    point(A0_SWAPPED)
    take_b0()
    a0.finish()
    point(A0_GATHERED)
    b0.half_sum()
    point(B0_SWAPPED)
    a0.collect()
    forward(xs[0, 0], attend(a0.part(0))[2], fs.at[0, 0])
    when_all(not_last, [shift_x[0]], "start")
    backward(0, 0, recompute(0, 0, a0.part(1), a0.scales[1]), a0.part(2))
    when_all(not_first, [shift_dy[0]], "start")
    keep_f[0].start()
    keep_g[0].start()
    point(A0_DONE)
    b0.finish()
    point(B0_GATHERED)
    b0.collect()
    point(B0_COLLECTED)
    forward(xs[1, 0], attend(b0.part(0))[2], fs.at[1, 0])
    when_all(not_last, [shift_x[1]], "start")
    backward(1, 0, recompute(1, 0, b0.part(1), b0.scales[1]), b0.part(2))
    when_all(not_first, [shift_dy[1]], "start")
    point(B0_DONE)

    when_all(not_first, [shift_x[0]], "wait_recv")
    when_all(not_last, [shift_dy[0]], "wait_recv")
    a1.start([raw_part(xs[0, 1]), kept_parts[1], dm_part(dys[0, 1])])
    point(A1_SCATTERED)
    when_all(not_first, [shift_x[1]], "wait_recv")
    when_all(not_last, [shift_dy[1]], "wait_recv")
    point(B1_HERE)
    send_kept[1].wait_recv()
    b1.start([raw_part(xs[1, 1]), raw_part(kept[1, 1]), dm_part(dys[1, 1])])
    point(B1_SCATTERED)
    a1.half_sum()
    b1.half_sum()
    point(B1_SWAPPED)
    a1.finish()
    b1.finish()
    point(B1_GATHERED)
    a1.collect()
    forward(xs[0, 1], attend(a1.part(0))[2], fs.at[0, 1])
    keep_f[1].start()
    backward(0, 1, recompute(0, 1, a1.part(1), a1.scales[1]), a1.part(2))
    keep_g[1].start()
    add_grads(0)
    b1.collect()
    point(B1_COLLECTED)
    forward(xs[1, 1], attend(b1.part(0))[2], fs.at[1, 1])
    point(F1_DONE)
    backward(1, 1, recompute(1, 1, b1.part(1), b1.scales[1]), b1.part(2))
    point(B1_DONE)
    add_grads(1)
    keep_down, keep_back = local(sum_down, g_down.at[0]), local(sum_back, g_back.at[0])
    keep_down.start()
    keep_back.start()

    for copy in keep_f + keep_g + [keep_down, keep_back]:
        copy.wait()
    for copy in send_kept:
        copy.wait_send()
    for item in rounds.values():
        item.drain()
    when_all(not_last, [send_xa], "wait_send")
    when_all(not_first, [send_dya], "wait_send")
    when_all(not_last, shift_x, "wait_send")
    when_all(not_first, shift_dy, "wait_send")
    when_all(x_far, [send_xb], "wait_send")
    when_all(dy_far, [send_dyb], "wait_send")
    for copy in out_f + out_g:
        copy.wait()


def hand_out(*refs):
    sources, targets, stages, sems = refs[:4], refs[4:8], refs[8:12], refs[12]
    loads, stores = [], []
    for source, target, stage in zip(sources, targets, stages, strict=True):
        for part in range(source.shape[0]):
            n = len(loads)
            loads.append(pltpu.make_async_copy(source.at[part], stage.at[part], sems.at[2 * n]))
            stores.append(pltpu.make_async_copy(stage.at[part], target.at[part], sems.at[2 * n + 1]))
    for load in loads:
        load.start()
    for load, store in zip(loads, stores, strict=True):
        load.wait()
        store.start()
    for store in stores:
        store.wait()


def solution(mesh):
    sections, shards = mesh.shape["pipe"], mesh.shape["tensor"]
    group = shards // 2
    rows = LAT // group

    def step(in_flight, entering, saved_inputs, latent_down, latent_back):
        local = latent_down.shape[1]
        act = pltpu.VMEM((2, 2, local, TOK), BF16)
        state = pltpu.VMEM((2, 2, LAT, TOK), BF16)
        buffers = []
        for kinds in ROUNDS.values():
            chunk = chunk_rows(kinds, rows)
            buffers += [
                pltpu.VMEM((group, chunk, TOK), BF16),
                pltpu.VMEM((group - 1, chunk, TOK), BF16),
                pltpu.VMEM((chunk, TOK), BF16),
                pltpu.VMEM((chunk, TOK), BF16),
                pltpu.VMEM((len(kinds), LAT, TOK), BF16),
            ]
        anywhere = pl.BlockSpec(memory_space=pl.ANY)
        results = (
            jax.ShapeDtypeStruct((2, 2, local, TOK), BF16),
            jax.ShapeDtypeStruct((2, 2, local, TOK), BF16),
            jax.ShapeDtypeStruct((1, local, LAT), BF16),
            jax.ShapeDtypeStruct((1, local, LAT), BF16),
        )
        made = pl.pallas_call(
            functools.partial(kernel, sections, shards),
            out_shape=results,
            in_specs=[anywhere] * 5,
            out_specs=[anywhere] * 4,
            scratch_shapes=[
                *[pltpu.VMEM((local, LAT), BF16)] * 2,
                *[pltpu.VMEM((LAT, local), BF16)] * 2,
                *[act] * 5,
                *[state] * 2,
                *[pltpu.VMEM((local, LAT), BF16)] * 2,
                *buffers,
                pltpu.SemaphoreType.DMA((N_REMOTE,)),
                pltpu.SemaphoreType.DMA((N_REMOTE,)),
                pltpu.SemaphoreType.DMA((N_LOCAL,)),
            ],
            compiler_params=pltpu.CompilerParams(
                collective_id=0, has_side_effects=True, vmem_limit_bytes=60 * 2**20
            ),
        )(
            jnp.swapaxes(in_flight, 1, 2),
            jnp.swapaxes(entering, 2, 3),
            jnp.swapaxes(saved_inputs, 2, 3),
            latent_down,
            jnp.swapaxes(latent_back, 1, 2),
        )
        outs, grads, grad_down, grad_back = pl.pallas_call(
            hand_out,
            out_shape=results,
            in_specs=[anywhere] * 4,
            out_specs=[anywhere] * 4,
            scratch_shapes=[
                *[pltpu.VMEM(result.shape, BF16) for result in results],
                pltpu.SemaphoreType.DMA((12,)),
            ],
            compiler_params=pltpu.CompilerParams(vmem_limit_bytes=60 * 2**20),
        )(*made)
        return (
            jnp.swapaxes(outs, 2, 3),
            jnp.swapaxes(grads, 2, 3),
            grad_down,
            jnp.swapaxes(grad_back, 1, 2),
        )

    return jax.shard_map(
        step,
        mesh=mesh,
        in_specs=(
            P(None, "pipe", "tensor"),
            P(None, None, None, "tensor"),
            P(None, None, "pipe", "tensor"),
            P("pipe", "tensor", None),
            P("pipe", None, "tensor"),
        ),
        out_specs=(
            P(None, None, "pipe", "tensor"),
            P(None, None, "pipe", "tensor"),
            P("pipe", "tensor", None),
            P("pipe", None, "tensor"),
        ),
        check_vma=False,
    )
```

```python
import functools

import jax
import jax.numpy as jnp
from jax import lax
from jax.experimental import pallas as pl
from jax.experimental.pallas import tpu as pltpu
from jax.sharding import PartitionSpec as P


MESH = pl.DeviceIdType.MESH
TOK = 128
LAT = 512
NORM_ROWS = 16
eps = 1e-06
F32 = jnp.float32
BF16 = jnp.bfloat16
NN = ((1,), (0,))
NT = ((1,), (1,))
TN = ((0,), (0,))

ROUNDS = {
    "a0": ("raw", "raw", "dm"),
    "b0": ("raw", "raw", "dm"),
    "a1": ("raw", "raw", "dm"),
    "b1": ("raw", "raw", "dm"),
}
N_LOCAL, N_REMOTE = 48, 160

(
    ENTERED, A0_HERE, A0_SCATTERED, A0_SWAPPED, A0_GATHERED, A0_DONE, B0_SCATTERED, B0_SWAPPED,
    B0_GATHERED, B0_COLLECTED, B0_DONE, A1_SCATTERED, B1_HERE, B1_SCATTERED, B1_SWAPPED,
    B1_GATHERED, B1_COLLECTED, F1_DONE, B1_DONE,
) = range(19)
SCHEDULE = {
    "in": (ENTERED, A0_SWAPPED, A0_SWAPPED, A0_HERE),
    "kept": (ENTERED, B0_GATHERED, B0_GATHERED, B0_GATHERED),
    "f0": (B1_COLLECTED, A1_SCATTERED, B0_DONE, B0_DONE),
    "g0": (B1_GATHERED, B1_GATHERED, B1_SWAPPED, B0_DONE),
    "f1": (F1_DONE, F1_DONE, F1_DONE, F1_DONE),
    "g1": (B1_DONE, B1_DONE, B1_DONE, B1_DONE),
}


def due(item, off, n):
    classes = [c for c, start in enumerate(SCHEDULE[item]) if start == n]
    if not classes:
        return None
    now = off == classes[0]
    for c in classes[1:]:
        now = now | (off == c)
    return now


def chunk_rows(kinds, rows):
    return rows * len(kinds) + NORM_ROWS * ("raw" in kinds)


def dot(a, b, over=NN):
    return lax.dot_general(a, b, (over, ((), ())), preferred_element_type=F32)


def norm_block(norms):
    row = lax.broadcasted_iota(jnp.int32, (NORM_ROWS, TOK), 0)
    block = jnp.zeros((NORM_ROWS, TOK), F32)
    for q, value in enumerate(norms):
        high = value.astype(BF16).astype(F32)
        block = jnp.where(row == 2 * q, high, jnp.where(row == 2 * q + 1, value - high, block))
    return block.astype(BF16)


def norms_of(block, count):
    return [block[2 * q : 2 * q + 1] + block[2 * q + 1 : 2 * q + 2] for q in range(count)]


def attend(latent):
    scores = dot(latent, latent, TN) * (4.0 / LAT)
    key = lax.broadcasted_iota(jnp.int32, scores.shape, 0)
    query = lax.broadcasted_iota(jnp.int32, scores.shape, 1)
    scores = jnp.where(query >= key, scores, -jnp.inf)
    weights = jnp.exp(scores - jnp.max(scores, axis=0, keepdims=True))
    probs = weights / jnp.sum(weights, axis=0, keepdims=True)
    probs_b = probs.astype(BF16)
    return probs, probs_b, dot(latent, probs_b).astype(BF16)


class Semaphores:
    def __init__(self, ref):
        self.ref, self.used = ref, 0

    def new(self):
        self.used += 1
        return self.ref.at[self.used - 1]


class Round:
    def __init__(self, kinds, refs, remote, mesh_at, width):
        self.kinds, self.width = kinds, width
        self.send, self.got, self.mine, self.other, self.full = refs
        self.pipe, self.half, self.j, self.group = mesh_at
        self.rows = LAT // self.group
        self.raws = sum(k == "raw" for k in kinds)
        j, group = self.j, self.group
        own = pl.ds(pl.multiple_of(j * self.rows, self.rows), self.rows)
        self.own = own
        self.scatter, self.gather, self.arrive = [], [], []
        self.relay, self.arrive_late = [], []

        def rows_of(device):
            return pl.ds(pl.multiple_of(device * self.rows, self.rows), self.rows)

        def arrival(out, part):
            return pltpu.make_async_remote_copy(
                src_ref=part,
                dst_ref=part,
                send_sem=out.src_sem,
                recv_sem=out.dst_sem,
                device_id=sibling,
                device_id_type=MESH,
            )

        for k in range(1, group):
            to = lax.rem(j + k, group)
            device = (self.pipe, self.half * group + to)
            self.scatter.append(remote(self.send.at[to], self.got.at[k - 1], device))
        other = j + 1 - 2 * lax.rem(j, 2)
        sibling = (self.pipe, self.half * group + other)
        mine = self.full.at[:, own, :]
        self.gather.append(remote(mine, mine, sibling))
        self.arrive_late.append(arrival(self.gather[0], self.full.at[:, rows_of(other), :]))
        for k in range(2, group, 2):
            to, source = lax.rem(j + k, group), lax.rem(j - k + group, group)
            out = remote(mine, mine, (self.pipe, self.half * group + to))
            self.gather.append(out)
            theirs = self.full.at[:, rows_of(source), :]
            self.arrive.append(arrival(out, theirs))
            self.relay.append(remote(theirs, theirs, sibling))
            far = self.full.at[:, rows_of(lax.rem(other - k + group, group)), :]
            self.arrive_late.append(arrival(self.relay[-1], far))
        self.swap = remote(self.mine, self.other, (self.pipe, (1 - self.half) * group + j))

    def start(self, parts):
        rows = self.rows
        norms = [norm for _, norm in parts if norm is not None]
        for p, (value, _) in enumerate(parts):
            value = value.astype(BF16)
            for g in range(self.group):
                self.send[g, p * rows : (p + 1) * rows] = value[g * rows : (g + 1) * rows]
        if norms:
            block = norm_block(norms)
            for g in range(self.group):
                self.send[g, len(parts) * rows :] = block
        for copy in self.scatter:
            copy.start()

    def half_sum(self):
        for copy in self.scatter:
            copy.wait_recv()
        total = self.send[self.j].astype(F32)
        for k in range(self.group - 1):
            total = total + self.got[k].astype(F32)
        last = len(self.kinds) * self.rows
        self.mine[:last] = total[:last].astype(BF16)
        if self.raws:
            self.mine[last:] = norm_block(norms_of(total[last:], self.raws))
        self.swap.start()

    def finish(self):
        self.swap.wait_recv()
        total = self.mine[...].astype(F32) + self.other[...].astype(F32)
        rows = self.rows
        scales, raw = self.scales_of(total), 0
        for p, kind in enumerate(self.kinds):
            value = total[p * rows : (p + 1) * rows]
            if kind == "raw":
                value = value * scales[raw]
                raw += 1
            self.full[p, self.own, :] = value.astype(BF16)
        for copy in self.gather:
            copy.start()

    def scales_of(self, total):
        norms = norms_of(total[len(self.kinds) * self.rows :], self.raws) if self.raws else []
        return [lax.rsqrt(norm / self.width + eps) for norm in norms]

    @property
    def scales(self):
        return self.scales_of(self.mine[...].astype(F32) + self.other[...].astype(F32))

    def collect(self):
        for copy, onward in zip(self.arrive, self.relay, strict=True):
            copy.wait_recv()
            onward.start()
        for copy in self.arrive_late:
            copy.wait_recv()

    def part(self, p):
        return self.full[p]

    def drain(self):
        for copy in self.scatter + self.gather + self.relay + [self.swap]:
            copy.wait_send()


def kernel(sections, shards, *refs):
    in_flight, entering, saved, down_in, back_in, outs, grads, g_down, g_back = refs[:9]
    down, back, down_t, back_t, xs, dys, kept, fs, gs, draws, mixes, sum_down, sum_back = refs[9:22]
    ssem, rsem, lsem = refs[-3:]
    buffers = refs[22:-3]
    group = shards // 2
    width = down.shape[0] * shards

    me = lax.axis_index("pipe")
    place = lax.axis_index("tensor")
    half, j = place // group, lax.rem(place, group)
    last = sections - 1
    sends, receives, locals_ = Semaphores(ssem), Semaphores(rsem), Semaphores(lsem)

    def remote(source, target, device):
        return pltpu.make_async_remote_copy(
            src_ref=source,
            dst_ref=target,
            send_sem=sends.new(),
            recv_sem=receives.new(),
            device_id=device,
            device_id_type=MESH,
        )

    def local(source, target):
        return pltpu.make_async_copy(source, target, locals_.new())

    not_first, not_last = me > 0, me < last
    nxt = (jnp.minimum(me + 1, last), place)
    prev = (jnp.maximum(me - 1, 0), place)
    across = (last - me, place)
    x_self, dy_self = me == sections // 2, me == sections // 2 - 1
    x_far = not_first & jnp.logical_not(x_self)
    dy_far = not_last & jnp.logical_not(dy_self)
    x_to = (jnp.where(x_far, sections - me, 0), place)
    dy_to = (jnp.where(dy_far, last - 1 - me, 0), place)

    load_down, load_back = local(down_in.at[0], down), local(back_in.at[0], back)
    load_kept = [local(saved.at[0, t], kept.at[0, t]) for t in range(2)]
    for copy in [load_down, load_back] + load_kept:
        copy.start()
    load_x = [local(entering.at[s, t], xs.at[s, t]) for s in range(2) for t in range(2)]
    load_dy = [local(entering.at[2 + s, t], dys.at[s, t]) for s in range(2) for t in range(2)]
    load_x_self = local(in_flight.at[1], xs.at[1, 0])
    load_dy_self = local(in_flight.at[3], dys.at[1, 0])

    def when_all(condition, copies, what):
        @pl.when(condition)
        def _():
            for copy in copies:
                getattr(copy, what)()

    when_all(me == 0, load_x, "start")
    when_all(me == last, load_dy, "start")
    when_all(x_self, [load_x_self], "start")
    when_all(dy_self, [load_dy_self], "start")

    def raw_part(x):
        wide = x.astype(F32)
        return dot(down_t[...], x), jnp.sum(wide * wide, axis=0, keepdims=True)

    barrier = pltpu.get_barrier_semaphore()

    def greet(device):
        pl.semaphore_signal(barrier, inc=1, device_id=device, device_id_type=MESH)

    for k in range(1, group):
        greet((me, half * group + lax.rem(j + k, group)))
    greet((me, (1 - half) * group + j))
    greet(across)
    count = group + 1
    for condition, device in ((not_last, nxt), (not_first, prev), (x_far, x_to), (dy_far, dy_to)):
        pl.when(condition)(functools.partial(greet, device))
        count = count + condition.astype(jnp.int32)
    load_down.wait()
    load_back.wait()
    down_t[...] = down[...].T
    back_t[...] = back[...].T
    for copy in load_kept:
        copy.wait()
    kept_parts = [raw_part(kept[0, t]) for t in range(2)]
    when_all(me == 0, load_x, "wait")
    when_all(me == last, load_dy, "wait")
    when_all(x_self, [load_x_self], "wait")
    when_all(dy_self, [load_dy_self], "wait")
    pl.semaphore_wait(barrier, count)

    send_xa = remote(in_flight.at[0], xs.at[0, 0], nxt)
    send_dya = remote(in_flight.at[2], dys.at[0, 0], prev)
    send_dyb = remote(in_flight.at[3], dys.at[1, 0], dy_to)
    send_kept = [remote(saved.at[1, t], kept.at[1, t], across) for t in range(2)]
    send_xb = remote(in_flight.at[1], xs.at[1, 0], x_to)
    when_all(not_last, [send_xa], "start")
    when_all(not_first, [send_dya], "start")
    at = (me, half, j, group)
    rounds = {}
    for n, (name, kinds) in enumerate(ROUNDS.items()):
        rounds[name] = Round(kinds, buffers[5 * n : 5 * n + 5], remote, at, width)

    def dm_part(dy):
        return dot(back_t[...], dy), None

    def forward(x, mixed, slot):
        slot[...] = (x.astype(F32) + dot(back[...], mixed)).astype(BF16)

    def backward(s, t, state, dmixed):
        latent, scale, probs, probs_b = state
        dprobs = dot(latent, dmixed, TN)
        dscores = probs * (dprobs - jnp.sum(probs * dprobs, axis=0, keepdims=True))
        dsym = ((dscores + dscores.T) * (4.0 / LAT)).astype(BF16)
        dlatent = dot(latent, dsym) + dot(dmixed, probs_b, NT)
        draw = (dlatent * scale).astype(BF16)
        draws[s, t] = draw
        along = jnp.sum(dlatent * latent.astype(F32), axis=0, keepdims=True)
        result = dys[s, t].astype(F32) + dot(down[...], draw)
        result = result - kept[s, t].astype(F32) * (scale * scale * along / width)
        gs[s, t] = result.astype(BF16)

    def recompute(s, t, latent, scale):
        probs, probs_b, mixed = attend(latent)
        mixes[s, t] = mixed
        return latent, scale, probs, probs_b

    def add_grads(s):
        for target, left, right in ((sum_down, kept, draws), (sum_back, dys, mixes)):
            total = dot(left[s, 0], right[s, 0], NT) + dot(left[s, 1], right[s, 1], NT)
            total = total.astype(BF16)
            if s == 1:
                total = (target[...].astype(F32) + total.astype(F32)).astype(BF16)
            target[...] = total

    shift_x = [remote(fs.at[s, 0], xs.at[s, 1], nxt) for s in range(2)]
    shift_dy = [remote(gs.at[s, 0], dys.at[s, 1], prev) for s in range(2)]
    out_f = [remote(fs.at[1, t], outs.at[1, t], across) for t in range(2)]
    out_g = [remote(gs.at[1, t], grads.at[1, t], across) for t in range(2)]
    keep_f = [local(fs.at[0, t], outs.at[0, t]) for t in range(2)]
    keep_g = [local(gs.at[0, t], grads.at[0, t]) for t in range(2)]

    off = jnp.where(me < sections // 2, sections // 2 - 1 - me, me - sections // 2) // max(sections // 8, 1)

    everyone = [(None, copy) for copy in send_kept]
    bulk = {
        "in": [(x_far, send_xb), (dy_far, send_dyb), everyone[0]],
        "kept": [everyone[1]],
        "f0": [(None, out_f[0])],
        "g0": [(None, out_g[0])],
        "f1": [(None, out_f[1])],
        "g1": [(None, out_g[1])],
    }

    def point(n):
        for item, copies in bulk.items():
            now = due(item, off, n)
            if now is None:
                continue

            @pl.when(now)
            def _():
                for condition, copy in copies:
                    if condition is None:
                        copy.start()
                    else:
                        when_all(condition, [copy], "start")

    a0, b0, a1, b1 = (rounds[name] for name in ROUNDS)

    def take_b0():
        when_all(x_far, [send_xb], "wait_recv")
        when_all(dy_far, [send_dyb], "wait_recv")
        send_kept[0].wait_recv()
        b0.start([raw_part(xs[1, 0]), raw_part(kept[1, 0]), dm_part(dys[1, 0])])
        point(B0_SCATTERED)

    point(ENTERED)
    when_all(not_first, [send_xa], "wait_recv")
    when_all(not_last, [send_dya], "wait_recv")
    point(A0_HERE)
    a0.start([raw_part(xs[0, 0]), kept_parts[0], dm_part(dys[0, 0])])
    point(A0_SCATTERED)
    a0.half_sum()
    point(A0_SWAPPED)
    take_b0()
    a0.finish()
    point(A0_GATHERED)
    b0.half_sum()
    point(B0_SWAPPED)
    a0.collect()
    forward(xs[0, 0], attend(a0.part(0))[2], fs.at[0, 0])
    when_all(not_last, [shift_x[0]], "start")
    backward(0, 0, recompute(0, 0, a0.part(1), a0.scales[1]), a0.part(2))
    when_all(not_first, [shift_dy[0]], "start")
    keep_f[0].start()
    keep_g[0].start()
    point(A0_DONE)
    b0.finish()
    point(B0_GATHERED)
    b0.collect()
    point(B0_COLLECTED)
    forward(xs[1, 0], attend(b0.part(0))[2], fs.at[1, 0])
    when_all(not_last, [shift_x[1]], "start")
    backward(1, 0, recompute(1, 0, b0.part(1), b0.scales[1]), b0.part(2))
    when_all(not_first, [shift_dy[1]], "start")
    point(B0_DONE)

    when_all(not_first, [shift_x[0]], "wait_recv")
    when_all(not_last, [shift_dy[0]], "wait_recv")
    a1.start([raw_part(xs[0, 1]), kept_parts[1], dm_part(dys[0, 1])])
    point(A1_SCATTERED)
    when_all(not_first, [shift_x[1]], "wait_recv")
    when_all(not_last, [shift_dy[1]], "wait_recv")
    point(B1_HERE)
    send_kept[1].wait_recv()
    b1.start([raw_part(xs[1, 1]), raw_part(kept[1, 1]), dm_part(dys[1, 1])])
    point(B1_SCATTERED)
    a1.half_sum()
    b1.half_sum()
    point(B1_SWAPPED)
    a1.finish()
    b1.finish()
    point(B1_GATHERED)
    a1.collect()
    forward(xs[0, 1], attend(a1.part(0))[2], fs.at[0, 1])
    keep_f[1].start()
    backward(0, 1, recompute(0, 1, a1.part(1), a1.scales[1]), a1.part(2))
    keep_g[1].start()
    add_grads(0)
    b1.collect()
    point(B1_COLLECTED)
    forward(xs[1, 1], attend(b1.part(0))[2], fs.at[1, 1])
    point(F1_DONE)
    backward(1, 1, recompute(1, 1, b1.part(1), b1.scales[1]), b1.part(2))
    point(B1_DONE)
    add_grads(1)
    keep_down, keep_back = local(sum_down, g_down.at[0]), local(sum_back, g_back.at[0])
    keep_down.start()
    keep_back.start()

    for copy in keep_f + keep_g + [keep_down, keep_back]:
        copy.wait()
    for copy in send_kept:
        copy.wait_send()
    for item in rounds.values():
        item.drain()
    when_all(not_last, [send_xa], "wait_send")
    when_all(not_first, [send_dya], "wait_send")
    when_all(not_last, shift_x, "wait_send")
    when_all(not_first, shift_dy, "wait_send")
    when_all(x_far, [send_xb], "wait_send")
    when_all(dy_far, [send_dyb], "wait_send")
    for copy in out_f + out_g:
        copy.wait()


def hand_out(*refs):
    sources, targets, stages, sems = refs[:4], refs[4:8], refs[8:12], refs[12]
    loads, stores = [], []
    for source, target, stage in zip(sources, targets, stages, strict=True):
        for part in range(source.shape[0]):
            n = len(loads)
            loads.append(pltpu.make_async_copy(source.at[part], stage.at[part], sems.at[2 * n]))
            stores.append(pltpu.make_async_copy(stage.at[part], target.at[part], sems.at[2 * n + 1]))
    for load in loads:
        load.start()
    for load, store in zip(loads, stores, strict=True):
        load.wait()
        store.start()
    for store in stores:
        store.wait()


def solution(mesh):
    sections, shards = mesh.shape["pipe"], mesh.shape["tensor"]
    group = shards // 2
    rows = LAT // group

    def step(in_flight, entering, saved_inputs, latent_down, latent_back):
        local = latent_down.shape[1]
        act = pltpu.VMEM((2, 2, local, TOK), BF16)
        state = pltpu.VMEM((2, 2, LAT, TOK), BF16)
        buffers = []
        for kinds in ROUNDS.values():
            chunk = chunk_rows(kinds, rows)
            buffers += [
                pltpu.VMEM((group, chunk, TOK), BF16),
                pltpu.VMEM((group - 1, chunk, TOK), BF16),
                pltpu.VMEM((chunk, TOK), BF16),
                pltpu.VMEM((chunk, TOK), BF16),
                pltpu.VMEM((len(kinds), LAT, TOK), BF16),
            ]
        anywhere = pl.BlockSpec(memory_space=pl.ANY)
        results = (
            jax.ShapeDtypeStruct((2, 2, local, TOK), BF16),
            jax.ShapeDtypeStruct((2, 2, local, TOK), BF16),
            jax.ShapeDtypeStruct((1, local, LAT), BF16),
            jax.ShapeDtypeStruct((1, local, LAT), BF16),
        )
        made = pl.pallas_call(
            functools.partial(kernel, sections, shards),
            out_shape=results,
            in_specs=[anywhere] * 5,
            out_specs=[anywhere] * 4,
            scratch_shapes=[
                *[pltpu.VMEM((local, LAT), BF16)] * 2,
                *[pltpu.VMEM((LAT, local), BF16)] * 2,
                *[act] * 5,
                *[state] * 2,
                *[pltpu.VMEM((local, LAT), BF16)] * 2,
                *buffers,
                pltpu.SemaphoreType.DMA((N_REMOTE,)),
                pltpu.SemaphoreType.DMA((N_REMOTE,)),
                pltpu.SemaphoreType.DMA((N_LOCAL,)),
            ],
            compiler_params=pltpu.CompilerParams(
                collective_id=0, has_side_effects=True, vmem_limit_bytes=60 * 2**20
            ),
        )(
            jnp.swapaxes(in_flight, 1, 2),
            jnp.swapaxes(entering, 2, 3),
            jnp.swapaxes(saved_inputs, 2, 3),
            latent_down,
            jnp.swapaxes(latent_back, 1, 2),
        )
        outs, grads, grad_down, grad_back = pl.pallas_call(
            hand_out,
            out_shape=results,
            in_specs=[anywhere] * 4,
            out_specs=[anywhere] * 4,
            scratch_shapes=[
                *[pltpu.VMEM(result.shape, BF16) for result in results],
                pltpu.SemaphoreType.DMA((12,)),
            ],
            compiler_params=pltpu.CompilerParams(vmem_limit_bytes=60 * 2**20),
        )(*made)
        return (
            jnp.swapaxes(outs, 2, 3),
            jnp.swapaxes(grads, 2, 3),
            grad_down,
            jnp.swapaxes(grad_back, 1, 2),
        )

    return jax.shard_map(
        step,
        mesh=mesh,
        in_specs=(
            P(None, "pipe", "tensor"),
            P(None, None, None, "tensor"),
            P(None, None, "pipe", "tensor"),
            P("pipe", "tensor", None),
            P("pipe", None, "tensor"),
        ),
        out_specs=(
            P(None, None, "pipe", "tensor"),
            P(None, None, "pipe", "tensor"),
            P("pipe", "tensor", None),
            P("pipe", None, "tensor"),
        ),
        check_vma=False,
    )
```

```python
import functools

import jax
import jax.numpy as jnp
from jax import lax
from jax.experimental import pallas as pl
from jax.experimental.pallas import tpu as pltpu
from jax.sharding import PartitionSpec as P


MESH = pl.DeviceIdType.MESH
TOK = 128
LAT = 512
NORM_ROWS = 16
eps = 1e-06
F32 = jnp.float32
BF16 = jnp.bfloat16
NN = ((1,), (0,))
NT = ((1,), (1,))
TN = ((0,), (0,))

ROUNDS = {
    "a0": ("raw", "raw", "dm"),
    "b0": ("raw", "raw", "dm"),
    "a1": ("raw", "raw", "dm"),
    "b1": ("raw", "raw", "dm"),
}
N_LOCAL, N_REMOTE = 48, 160

(
    ENTERED, A0_HERE, A0_SCATTERED, A0_SWAPPED, A0_GATHERED, A0_DONE, B0_SCATTERED, B0_SWAPPED,
    B0_GATHERED, B0_COLLECTED, B0_DONE, A1_SCATTERED, B1_HERE, B1_SCATTERED, B1_SWAPPED,
    B1_GATHERED, B1_COLLECTED, F1_DONE, B1_DONE,
) = range(19)
SCHEDULE = {
    "in": (ENTERED, A0_SWAPPED, A0_SWAPPED, A0_SCATTERED),
    "kept": (ENTERED, B0_GATHERED, B0_GATHERED, B0_GATHERED),
    "f0": (A1_SCATTERED, B1_SWAPPED, B1_GATHERED, B0_DONE),
    "g0": (B1_GATHERED, B1_GATHERED, B1_GATHERED, B1_GATHERED),
    "f1": (F1_DONE, F1_DONE, F1_DONE, F1_DONE),
    "g1": (B1_DONE, B1_DONE, B1_DONE, B1_DONE),
}


def due(item, off, n):
    classes = [c for c, start in enumerate(SCHEDULE[item]) if start == n]
    if not classes:
        return None
    now = off == classes[0]
    for c in classes[1:]:
        now = now | (off == c)
    return now


def chunk_rows(kinds, rows):
    return rows * len(kinds) + NORM_ROWS * ("raw" in kinds)


def dot(a, b, over=NN):
    return lax.dot_general(a, b, (over, ((), ())), preferred_element_type=F32)


def norm_block(norms):
    row = lax.broadcasted_iota(jnp.int32, (NORM_ROWS, TOK), 0)
    block = jnp.zeros((NORM_ROWS, TOK), F32)
    for q, value in enumerate(norms):
        high = value.astype(BF16).astype(F32)
        block = jnp.where(row == 2 * q, high, jnp.where(row == 2 * q + 1, value - high, block))
    return block.astype(BF16)


def norms_of(block, count):
    return [block[2 * q : 2 * q + 1] + block[2 * q + 1 : 2 * q + 2] for q in range(count)]


def attend(latent):
    scores = dot(latent, latent, TN) * (4.0 / LAT)
    key = lax.broadcasted_iota(jnp.int32, scores.shape, 0)
    query = lax.broadcasted_iota(jnp.int32, scores.shape, 1)
    scores = jnp.where(query >= key, scores, -jnp.inf)
    weights = jnp.exp(scores - jnp.max(scores, axis=0, keepdims=True))
    probs = weights / jnp.sum(weights, axis=0, keepdims=True)
    probs_b = probs.astype(BF16)
    return probs, probs_b, dot(latent, probs_b).astype(BF16)


class Semaphores:
    def __init__(self, ref):
        self.ref, self.used = ref, 0

    def new(self):
        self.used += 1
        return self.ref.at[self.used - 1]


class Round:
    def __init__(self, kinds, refs, remote, mesh_at, width):
        self.kinds, self.width = kinds, width
        self.send, self.got, self.mine, self.other, self.full = refs
        self.pipe, self.half, self.j, self.group = mesh_at
        self.rows = LAT // self.group
        self.raws = sum(k == "raw" for k in kinds)
        j, group = self.j, self.group
        own = pl.ds(pl.multiple_of(j * self.rows, self.rows), self.rows)
        self.own = own
        self.scatter, self.gather, self.arrive = [], [], []
        self.relay, self.arrive_late = [], []

        def rows_of(device):
            return pl.ds(pl.multiple_of(device * self.rows, self.rows), self.rows)

        def arrival(out, part):
            return pltpu.make_async_remote_copy(
                src_ref=part,
                dst_ref=part,
                send_sem=out.src_sem,
                recv_sem=out.dst_sem,
                device_id=sibling,
                device_id_type=MESH,
            )

        for k in range(1, group):
            to = lax.rem(j + k, group)
            device = (self.pipe, self.half * group + to)
            self.scatter.append(remote(self.send.at[to], self.got.at[k - 1], device))
        other = j + 1 - 2 * lax.rem(j, 2)
        sibling = (self.pipe, self.half * group + other)
        mine = self.full.at[:, own, :]
        self.gather.append(remote(mine, mine, sibling))
        self.arrive_late.append(arrival(self.gather[0], self.full.at[:, rows_of(other), :]))
        for k in range(2, group, 2):
            to, source = lax.rem(j + k, group), lax.rem(j - k + group, group)
            out = remote(mine, mine, (self.pipe, self.half * group + to))
            self.gather.append(out)
            theirs = self.full.at[:, rows_of(source), :]
            self.arrive.append(arrival(out, theirs))
            self.relay.append(remote(theirs, theirs, sibling))
            far = self.full.at[:, rows_of(lax.rem(other - k + group, group)), :]
            self.arrive_late.append(arrival(self.relay[-1], far))
        self.swap = remote(self.mine, self.other, (self.pipe, (1 - self.half) * group + j))

    def start(self, parts):
        rows = self.rows
        norms = [norm for _, norm in parts if norm is not None]
        for p, (value, _) in enumerate(parts):
            value = value.astype(BF16)
            for g in range(self.group):
                self.send[g, p * rows : (p + 1) * rows] = value[g * rows : (g + 1) * rows]
        if norms:
            block = norm_block(norms)
            for g in range(self.group):
                self.send[g, len(parts) * rows :] = block
        for copy in self.scatter:
            copy.start()

    def half_sum(self):
        for copy in self.scatter:
            copy.wait_recv()
        total = self.send[self.j].astype(F32)
        for k in range(self.group - 1):
            total = total + self.got[k].astype(F32)
        last = len(self.kinds) * self.rows
        self.mine[:last] = total[:last].astype(BF16)
        if self.raws:
            self.mine[last:] = norm_block(norms_of(total[last:], self.raws))
        self.swap.start()

    def finish(self):
        self.swap.wait_recv()
        total = self.mine[...].astype(F32) + self.other[...].astype(F32)
        rows = self.rows
        scales, raw = self.scales_of(total), 0
        for p, kind in enumerate(self.kinds):
            value = total[p * rows : (p + 1) * rows]
            if kind == "raw":
                value = value * scales[raw]
                raw += 1
            self.full[p, self.own, :] = value.astype(BF16)
        for copy in self.gather:
            copy.start()

    def scales_of(self, total):
        norms = norms_of(total[len(self.kinds) * self.rows :], self.raws) if self.raws else []
        return [lax.rsqrt(norm / self.width + eps) for norm in norms]

    @property
    def scales(self):
        return self.scales_of(self.mine[...].astype(F32) + self.other[...].astype(F32))

    def collect(self):
        for copy, onward in zip(self.arrive, self.relay, strict=True):
            copy.wait_recv()
            onward.start()
        for copy in self.arrive_late:
            copy.wait_recv()

    def part(self, p):
        return self.full[p]

    def drain(self):
        for copy in self.scatter + self.gather + self.relay + [self.swap]:
            copy.wait_send()


def kernel(sections, shards, *refs):
    in_flight, entering, saved, down_in, back_in, outs, grads, g_down, g_back = refs[:9]
    down, back, down_t, back_t, xs, dys, kept, fs, gs, draws, mixes, sum_down, sum_back = refs[9:22]
    ssem, rsem, lsem = refs[-3:]
    buffers = refs[22:-3]
    group = shards // 2
    width = down.shape[0] * shards

    me = lax.axis_index("pipe")
    place = lax.axis_index("tensor")
    half, j = place // group, lax.rem(place, group)
    last = sections - 1
    sends, receives, locals_ = Semaphores(ssem), Semaphores(rsem), Semaphores(lsem)

    def remote(source, target, device):
        return pltpu.make_async_remote_copy(
            src_ref=source,
            dst_ref=target,
            send_sem=sends.new(),
            recv_sem=receives.new(),
            device_id=device,
            device_id_type=MESH,
        )

    def local(source, target):
        return pltpu.make_async_copy(source, target, locals_.new())

    not_first, not_last = me > 0, me < last
    nxt = (jnp.minimum(me + 1, last), place)
    prev = (jnp.maximum(me - 1, 0), place)
    across = (last - me, place)
    x_self, dy_self = me == sections // 2, me == sections // 2 - 1
    x_far = not_first & jnp.logical_not(x_self)
    dy_far = not_last & jnp.logical_not(dy_self)
    x_to = (jnp.where(x_far, sections - me, 0), place)
    dy_to = (jnp.where(dy_far, last - 1 - me, 0), place)

    load_down, load_back = local(down_in.at[0], down), local(back_in.at[0], back)
    load_kept = [local(saved.at[0, t], kept.at[0, t]) for t in range(2)]
    for copy in [load_down, load_back] + load_kept:
        copy.start()
    load_x = [local(entering.at[s, t], xs.at[s, t]) for s in range(2) for t in range(2)]
    load_dy = [local(entering.at[2 + s, t], dys.at[s, t]) for s in range(2) for t in range(2)]
    load_x_self = local(in_flight.at[1], xs.at[1, 0])
    load_dy_self = local(in_flight.at[3], dys.at[1, 0])

    def when_all(condition, copies, what):
        @pl.when(condition)
        def _():
            for copy in copies:
                getattr(copy, what)()

    when_all(me == 0, load_x, "start")
    when_all(me == last, load_dy, "start")
    when_all(x_self, [load_x_self], "start")
    when_all(dy_self, [load_dy_self], "start")

    def raw_part(x):
        wide = x.astype(F32)
        return dot(down_t[...], x), jnp.sum(wide * wide, axis=0, keepdims=True)

    barrier = pltpu.get_barrier_semaphore()

    def greet(device):
        pl.semaphore_signal(barrier, inc=1, device_id=device, device_id_type=MESH)

    for k in range(1, group):
        greet((me, half * group + lax.rem(j + k, group)))
    greet((me, (1 - half) * group + j))
    greet(across)
    count = group + 1
    for condition, device in ((not_last, nxt), (not_first, prev), (x_far, x_to), (dy_far, dy_to)):
        pl.when(condition)(functools.partial(greet, device))
        count = count + condition.astype(jnp.int32)
    load_down.wait()
    load_back.wait()
    down_t[...] = down[...].T
    back_t[...] = back[...].T
    for copy in load_kept:
        copy.wait()
    kept_parts = [raw_part(kept[0, t]) for t in range(2)]
    when_all(me == 0, load_x, "wait")
    when_all(me == last, load_dy, "wait")
    when_all(x_self, [load_x_self], "wait")
    when_all(dy_self, [load_dy_self], "wait")
    pl.semaphore_wait(barrier, count)

    send_xa = remote(in_flight.at[0], xs.at[0, 0], nxt)
    send_dya = remote(in_flight.at[2], dys.at[0, 0], prev)
    send_dyb = remote(in_flight.at[3], dys.at[1, 0], dy_to)
    send_kept = [remote(saved.at[1, t], kept.at[1, t], across) for t in range(2)]
    send_xb = remote(in_flight.at[1], xs.at[1, 0], x_to)
    when_all(not_last, [send_xa], "start")
    when_all(not_first, [send_dya], "start")
    at = (me, half, j, group)
    rounds = {}
    for n, (name, kinds) in enumerate(ROUNDS.items()):
        rounds[name] = Round(kinds, buffers[5 * n : 5 * n + 5], remote, at, width)

    def dm_part(dy):
        return dot(back_t[...], dy), None

    def forward(x, mixed, slot):
        slot[...] = (x.astype(F32) + dot(back[...], mixed)).astype(BF16)

    def backward(s, t, state, dmixed):
        latent, scale, probs, probs_b = state
        dprobs = dot(latent, dmixed, TN)
        dscores = probs * (dprobs - jnp.sum(probs * dprobs, axis=0, keepdims=True))
        dsym = ((dscores + dscores.T) * (4.0 / LAT)).astype(BF16)
        dlatent = dot(latent, dsym) + dot(dmixed, probs_b, NT)
        draw = (dlatent * scale).astype(BF16)
        draws[s, t] = draw
        along = jnp.sum(dlatent * latent.astype(F32), axis=0, keepdims=True)
        result = dys[s, t].astype(F32) + dot(down[...], draw)
        result = result - kept[s, t].astype(F32) * (scale * scale * along / width)
        gs[s, t] = result.astype(BF16)

    def recompute(s, t, latent, scale):
        probs, probs_b, mixed = attend(latent)
        mixes[s, t] = mixed
        return latent, scale, probs, probs_b

    def add_grads(s):
        for target, left, right in ((sum_down, kept, draws), (sum_back, dys, mixes)):
            total = dot(left[s, 0], right[s, 0], NT) + dot(left[s, 1], right[s, 1], NT)
            total = total.astype(BF16)
            if s == 1:
                total = (target[...].astype(F32) + total.astype(F32)).astype(BF16)
            target[...] = total

    shift_x = [remote(fs.at[s, 0], xs.at[s, 1], nxt) for s in range(2)]
    shift_dy = [remote(gs.at[s, 0], dys.at[s, 1], prev) for s in range(2)]
    out_f = [remote(fs.at[1, t], outs.at[1, t], across) for t in range(2)]
    out_g = [remote(gs.at[1, t], grads.at[1, t], across) for t in range(2)]
    keep_f = [local(fs.at[0, t], outs.at[0, t]) for t in range(2)]
    keep_g = [local(gs.at[0, t], grads.at[0, t]) for t in range(2)]

    off = jnp.where(me < sections // 2, sections // 2 - 1 - me, me - sections // 2) // max(sections // 8, 1)

    everyone = [(None, copy) for copy in send_kept]
    bulk = {
        "in": [(x_far, send_xb), (dy_far, send_dyb), everyone[0]],
        "kept": [everyone[1]],
        "f0": [(None, out_f[0])],
        "g0": [(None, out_g[0])],
        "f1": [(None, out_f[1])],
        "g1": [(None, out_g[1])],
    }

    def point(n):
        for item, copies in bulk.items():
            now = due(item, off, n)
            if now is None:
                continue

            @pl.when(now)
            def _():
                for condition, copy in copies:
                    if condition is None:
                        copy.start()
                    else:
                        when_all(condition, [copy], "start")

    a0, b0, a1, b1 = (rounds[name] for name in ROUNDS)

    def take_b0():
        when_all(x_far, [send_xb], "wait_recv")
        when_all(dy_far, [send_dyb], "wait_recv")
        send_kept[0].wait_recv()
        b0.start([raw_part(xs[1, 0]), raw_part(kept[1, 0]), dm_part(dys[1, 0])])
        point(B0_SCATTERED)

    point(ENTERED)
    when_all(not_first, [send_xa], "wait_recv")
    when_all(not_last, [send_dya], "wait_recv")
    point(A0_HERE)
    a0.start([raw_part(xs[0, 0]), kept_parts[0], dm_part(dys[0, 0])])
    point(A0_SCATTERED)
    a0.half_sum()
    point(A0_SWAPPED)
    take_b0()
    a0.finish()
    point(A0_GATHERED)
    b0.half_sum()
    point(B0_SWAPPED)
    a0.collect()
    forward(xs[0, 0], attend(a0.part(0))[2], fs.at[0, 0])
    when_all(not_last, [shift_x[0]], "start")
    backward(0, 0, recompute(0, 0, a0.part(1), a0.scales[1]), a0.part(2))
    when_all(not_first, [shift_dy[0]], "start")
    keep_f[0].start()
    keep_g[0].start()
    point(A0_DONE)
    b0.finish()
    point(B0_GATHERED)
    b0.collect()
    point(B0_COLLECTED)
    forward(xs[1, 0], attend(b0.part(0))[2], fs.at[1, 0])
    when_all(not_last, [shift_x[1]], "start")
    backward(1, 0, recompute(1, 0, b0.part(1), b0.scales[1]), b0.part(2))
    when_all(not_first, [shift_dy[1]], "start")
    point(B0_DONE)

    when_all(not_first, [shift_x[0]], "wait_recv")
    when_all(not_last, [shift_dy[0]], "wait_recv")
    a1.start([raw_part(xs[0, 1]), kept_parts[1], dm_part(dys[0, 1])])
    point(A1_SCATTERED)
    when_all(not_first, [shift_x[1]], "wait_recv")
    when_all(not_last, [shift_dy[1]], "wait_recv")
    point(B1_HERE)
    send_kept[1].wait_recv()
    b1.start([raw_part(xs[1, 1]), raw_part(kept[1, 1]), dm_part(dys[1, 1])])
    point(B1_SCATTERED)
    a1.half_sum()
    b1.half_sum()
    point(B1_SWAPPED)
    a1.finish()
    b1.finish()
    point(B1_GATHERED)
    a1.collect()
    forward(xs[0, 1], attend(a1.part(0))[2], fs.at[0, 1])
    keep_f[1].start()
    backward(0, 1, recompute(0, 1, a1.part(1), a1.scales[1]), a1.part(2))
    keep_g[1].start()
    add_grads(0)
    b1.collect()
    point(B1_COLLECTED)
    forward(xs[1, 1], attend(b1.part(0))[2], fs.at[1, 1])
    point(F1_DONE)
    backward(1, 1, recompute(1, 1, b1.part(1), b1.scales[1]), b1.part(2))
    point(B1_DONE)
    add_grads(1)
    keep_down, keep_back = local(sum_down, g_down.at[0]), local(sum_back, g_back.at[0])
    keep_down.start()
    keep_back.start()

    for copy in keep_f + keep_g + [keep_down, keep_back]:
        copy.wait()
    for copy in send_kept:
        copy.wait_send()
    for item in rounds.values():
        item.drain()
    when_all(not_last, [send_xa], "wait_send")
    when_all(not_first, [send_dya], "wait_send")
    when_all(not_last, shift_x, "wait_send")
    when_all(not_first, shift_dy, "wait_send")
    when_all(x_far, [send_xb], "wait_send")
    when_all(dy_far, [send_dyb], "wait_send")
    for copy in out_f + out_g:
        copy.wait()


def hand_out(*refs):
    sources, targets, stages, sems = refs[:4], refs[4:8], refs[8:12], refs[12]
    loads, stores = [], []
    for source, target, stage in zip(sources, targets, stages, strict=True):
        for part in range(source.shape[0]):
            n = len(loads)
            loads.append(pltpu.make_async_copy(source.at[part], stage.at[part], sems.at[2 * n]))
            stores.append(pltpu.make_async_copy(stage.at[part], target.at[part], sems.at[2 * n + 1]))
    for load in loads:
        load.start()
    for load, store in zip(loads, stores, strict=True):
        load.wait()
        store.start()
    for store in stores:
        store.wait()


def solution(mesh):
    sections, shards = mesh.shape["pipe"], mesh.shape["tensor"]
    group = shards // 2
    rows = LAT // group

    def step(in_flight, entering, saved_inputs, latent_down, latent_back):
        local = latent_down.shape[1]
        act = pltpu.VMEM((2, 2, local, TOK), BF16)
        state = pltpu.VMEM((2, 2, LAT, TOK), BF16)
        buffers = []
        for kinds in ROUNDS.values():
            chunk = chunk_rows(kinds, rows)
            buffers += [
                pltpu.VMEM((group, chunk, TOK), BF16),
                pltpu.VMEM((group - 1, chunk, TOK), BF16),
                pltpu.VMEM((chunk, TOK), BF16),
                pltpu.VMEM((chunk, TOK), BF16),
                pltpu.VMEM((len(kinds), LAT, TOK), BF16),
            ]
        anywhere = pl.BlockSpec(memory_space=pl.ANY)
        results = (
            jax.ShapeDtypeStruct((2, 2, local, TOK), BF16),
            jax.ShapeDtypeStruct((2, 2, local, TOK), BF16),
            jax.ShapeDtypeStruct((1, local, LAT), BF16),
            jax.ShapeDtypeStruct((1, local, LAT), BF16),
        )
        made = pl.pallas_call(
            functools.partial(kernel, sections, shards),
            out_shape=results,
            in_specs=[anywhere] * 5,
            out_specs=[anywhere] * 4,
            scratch_shapes=[
                *[pltpu.VMEM((local, LAT), BF16)] * 2,
                *[pltpu.VMEM((LAT, local), BF16)] * 2,
                *[act] * 5,
                *[state] * 2,
                *[pltpu.VMEM((local, LAT), BF16)] * 2,
                *buffers,
                pltpu.SemaphoreType.DMA((N_REMOTE,)),
                pltpu.SemaphoreType.DMA((N_REMOTE,)),
                pltpu.SemaphoreType.DMA((N_LOCAL,)),
            ],
            compiler_params=pltpu.CompilerParams(
                collective_id=0, has_side_effects=True, vmem_limit_bytes=60 * 2**20
            ),
        )(
            jnp.swapaxes(in_flight, 1, 2),
            jnp.swapaxes(entering, 2, 3),
            jnp.swapaxes(saved_inputs, 2, 3),
            latent_down,
            jnp.swapaxes(latent_back, 1, 2),
        )
        outs, grads, grad_down, grad_back = pl.pallas_call(
            hand_out,
            out_shape=results,
            in_specs=[anywhere] * 4,
            out_specs=[anywhere] * 4,
            scratch_shapes=[
                *[pltpu.VMEM(result.shape, BF16) for result in results],
                pltpu.SemaphoreType.DMA((12,)),
            ],
            compiler_params=pltpu.CompilerParams(vmem_limit_bytes=60 * 2**20),
        )(*made)
        return (
            jnp.swapaxes(outs, 2, 3),
            jnp.swapaxes(grads, 2, 3),
            grad_down,
            jnp.swapaxes(grad_back, 1, 2),
        )

    return jax.shard_map(
        step,
        mesh=mesh,
        in_specs=(
            P(None, "pipe", "tensor"),
            P(None, None, None, "tensor"),
            P(None, None, "pipe", "tensor"),
            P("pipe", "tensor", None),
            P("pipe", None, "tensor"),
        ),
        out_specs=(
            P(None, None, "pipe", "tensor"),
            P(None, None, "pipe", "tensor"),
            P("pipe", "tensor", None),
            P("pipe", None, "tensor"),
        ),
        check_vma=False,
    )
```
